32 devices in a mesh: groups: 2 (over y), gx: 4 (over x, core), gy: 4 (over z).
Axes of the slice: x: 2, y: 2, z: 4, core: 2. Of those that a mesh axis runs over, the one named last changes fastest.
Arguments:
- layer_input: bfloat16 [384, 16384], P(('groups', 'gx'), 'gy'), parts along dimension 0, may hold values from -0.4375 to 0.4375
- packed_weight: bfloat16 [16384, 10240], P('gy', 'gx'), may hold values from -0.046875 to 0.046875
- packed_cotangent: bfloat16 [384, 10240], P(('groups', 'gy'), 'gx'), parts along dimension 0, may hold values from -8 to 8
- context: bfloat16 [384, 8192], P(('groups', 'gx'), 'gy'), parts along dimension 0, may hold values from -0.4375 to 0.4375
- mixing_weight: bfloat16 [8192, 16384], P('gy', 'gx'), may hold values from -0.0625 to 0.0625
- mixing_cotangent: bfloat16 [384, 16384], P(('groups', 'gy'), 'gx'), parts along dimension 0, may hold values from -8 to 8
Outputs:
- input_gradient: bfloat16 [384, 16384], P(('groups', 'gx'), 'gy'), parts along dimension 0
- packed_gradient: bfloat16 [32768, 10240], P(('groups', 'gy'), 'gx'), parts along dimension 0
- context_gradient: bfloat16 [384, 8192], P(('groups', 'gx'), 'gy'), parts along dimension 0
- mixing_gradient: bfloat16 [16384, 16384], P(('groups', 'gy'), 'gx'), parts along dimension 0
The draws below stay inside these ranges and needn't reach their ends.
There are 2 independent parts, one for each index of `groups`. The reference program is written for one: setup_inputs(seed, part) draws one part's arguments, and reference() takes and returns one part's arrays. A program takes and returns all parts, laid end to end along the dimension named above; an argument that names none is the same for every part. Nothing has to cross between parts.
All inputs are finite; a program needn't handle non-finite values.
Results may differ from the reference program's by a relative error of at most 0.009.
Values may be sent and summed in bfloat16 or wider, within the bound.
A program may use at most 192 MiB of HBM per device.

```python
import jax
import jax.numpy as jnp
from jax import lax

D = 16384
PACKED = 10240
CONTEXT = 8192
TOKENS = 192
N_GX = 4


def raised(values, key, source, target, parts, factor):
    owner, partner = [(jnp.arange(values.shape[dim]) // (values.shape[dim] // parts)).reshape([-1 if axis == dim else 1 for axis in range(values.ndim)]) for dim in (source, target)]
    chosen = jax.random.permutation(key, parts)[partner]
    strong = (owner == chosen) | (owner == (partner + parts // 2) % parts)
    return jnp.where(strong, factor * values, values)


def levels(own_key, dims, pieces, smallest, top_value):
    def one(axis_at, blocks):
        heights = jax.random.uniform(jax.random.fold_in(jax.random.fold_in(own_key, 6), axis_at), (blocks,), jnp.float32, smallest / len(pieces), top_value / len(pieces))
        return jnp.repeat(jnp.exp(heights), dims[axis_at] // blocks).reshape((-1,) + (1,) * (len(dims) - axis_at - 1))

    gain = one(*pieces[0])
    for cut in pieces[1:]:
        gain = gain * one(*cut)
    return gain


def scatter_about(rng, shape, scale, reach, shards=(), kind=jnp.bfloat16):
    drawn = jax.random.normal(rng, shape, jnp.float32) * scale
    if len(shards) > 0:
        drawn = levels(rng, shape, shards, -0.22, 0.18) * drawn
    return jnp.clip(drawn, min=-reach, max=reach).astype(kind)


def gaussian_with(rng, shape, deviation, limit, split, heavy, dtype=jnp.bfloat16):
    values = deviation * jax.random.normal(rng, shape, jnp.float32)
    if split:
        values = values * levels(rng, shape, split, -0.22, 0.18)
    return jnp.clip(raised(values, jax.random.fold_in(rng, 3), *heavy), -limit, limit).astype(dtype)


def setup_inputs(seed: int = 0, part: int = 0) -> dict:
    key_of = jax.random.split(jax.random.key(seed), 7)
    own_keys = jax.random.split(jax.random.fold_in(key_of[6], part), 7)
    return {
        "layer_input": scatter_about(own_keys[0], (TOKENS, D), (TOKENS ** -0.5), 0.4375, ((0, 4), (1, 4))),
        "packed_weight": scatter_about(key_of[1], (D, PACKED), D ** -0.5, 0.046875, ((0, 4), (1, 4))),
        "packed_cotangent": gaussian_with(own_keys[2], (TOKENS, PACKED), 1.0, 8.0, ((0, 4), (1, 4)), (1, 0, 4, 2.0)),
        "context": scatter_about(own_keys[3], (TOKENS, CONTEXT), (TOKENS ** -0.5), 0.4375, ((0, 4), (1, 4))),
        "mixing_weight": scatter_about(key_of[4], (CONTEXT, D), CONTEXT ** -0.5, 0.0625, ((0, 4), (1, 4))),
        "mixing_cotangent": gaussian_with(own_keys[5], (TOKENS, D), 1.0, 8.0, ((0, 4), (1, 4)), (1, 0, 4, 2.0)),
    }


def panel_sum(cotangent, weight, panels):
    width = cotangent.shape[1] // panels

    def add_panel(index, total):
        left = lax.dynamic_slice_in_dim(cotangent, index * width, width, 1)
        right = lax.dynamic_slice_in_dim(weight, index * width, width, 1)
        term = lax.dot_general(left, right, (((1,), (1,)), ((), ())), preferred_element_type=jnp.float32)
        rounded = lax.optimization_barrier(term.astype(jnp.bfloat16))
        return total + rounded.astype(jnp.float32)

    start_total = jnp.zeros((cotangent.shape[0], weight.shape[0]), jnp.float32)
    total = lax.fori_loop(0, panels, add_panel, start_total)
    return total.astype(jnp.bfloat16)


def reference(layer_input, packed_weight, packed_cotangent, context, mixing_weight, mixing_cotangent):
    packed_gradient = jnp.dot(layer_input.T, packed_cotangent, preferred_element_type=jnp.float32).astype(jnp.bfloat16)
    mixing_gradient = jnp.dot(context.T, mixing_cotangent, preferred_element_type=jnp.float32).astype(jnp.bfloat16)
    input_gradient = panel_sum(packed_cotangent, packed_weight, N_GX)
    context_gradient = panel_sum(mixing_cotangent, mixing_weight, N_GX)
    return input_gradient, packed_gradient, context_gradient, mixing_gradient
```

```python
import functools

import jax
import jax.numpy as jnp
from jax import lax
from jax.experimental import pallas as pl
from jax.experimental.pallas import tpu as pltpu
from jax.sharding import PartitionSpec as P

BF16 = jnp.bfloat16
F32 = jnp.float32
MESH = pl.DeviceIdType.MESH
ANY = pl.ANY
AHEAD = 3


def exchange_kernel(
    n_gx, n_gy, g_chunks, h_chunks,
    x_in, w_in, g_in, c_in, m_in, h_in,
    xt_out, ct_out, gall_out, hall_out, dx_out, dc_out,
    wv, mv, gall, hall, xall, call, xt, ct, acc_x, acc_c,
    term_x, part_x, pair_x, cross_x, res_x,
    term_c, part_c, pair_c, cross_c, res_c,
    w_sem, m_sem, own_sem, g_send, g_recv, h_send, h_recv,
    xs_send, xs_recv, cs_send, cs_recv,
    px_send, px_recv, cx_send, cx_recv, pc_send, pc_recv, cc_send, cc_recv,
    out_sem,
):
    gx = lax.axis_index("gx")
    z = lax.axis_index("gy")
    core = lax.rem(gx, 2)
    chip = gx // 2
    partner = gx + 1 - 2 * core
    n_chips = n_gx // 2
    g_width = g_in.shape[1] // g_chunks
    h_width = h_in.shape[1] // h_chunks
    rows = g_in.shape[0]
    tokens = rows * n_gy

    def peer(s):
        return 2 * lax.rem(chip + s, n_chips) + core

    loads_w = [
        pltpu.make_async_copy(w_in.at[:, pl.ds(c * g_width, g_width)], wv.at[c], w_sem.at[c])
        for c in range(g_chunks)
    ]
    loads_m = [
        pltpu.make_async_copy(m_in.at[:, pl.ds(c * h_width, h_width)], mv.at[c], m_sem.at[c])
        for c in range(h_chunks)
    ]
    own = [
        pltpu.make_async_copy(g_in, gall.at[z], own_sem.at[0]),
        pltpu.make_async_copy(h_in, hall.at[z], own_sem.at[1]),
        pltpu.make_async_copy(x_in, xall.at[gx], own_sem.at[2]),
        pltpu.make_async_copy(c_in, call.at[gx], own_sem.at[3]),
    ]
    for copy in own:
        copy.start()
    for copy in loads_w:
        copy.start()
    for copy in loads_m:
        copy.start()

    barrier = pltpu.get_barrier_semaphore()

    def greet(**where):
        pl.semaphore_signal(barrier, inc=1, device_id=where, device_id_type=MESH)

    greet(gx=partner)
    for s in range(1, n_chips):
        greet(gx=peer(s))

    @pl.when(z > 0)
    def _():
        greet(gy=z - 1)

    @pl.when(z < n_gy - 1)
    def _():
        greet(gy=z + 1)

    ends = jnp.where(z > 0, 1, 0) + jnp.where(z < n_gy - 1, 1, 0)
    pl.semaphore_wait(barrier, n_chips + ends)

    chunks = [("g", c) for c in range(g_chunks)] + [("h", c) for c in range(h_chunks)]

    def chain_copy(kind, c, way, block, source=None):
        if kind == "g":
            buf, send, recv, width = gall, g_send, g_recv, g_width
        else:
            buf, send, recv, width = hall, h_send, h_recv, h_width
        columns = pl.ds(c * width, width)
        src = buf.at[block, :, columns] if source is None else source.at[:, columns]
        return pltpu.make_async_remote_copy(
            src_ref=src,
            dst_ref=buf.at[block, :, columns],
            send_sem=send.at[way, block, c],
            recv_sem=recv.at[block, c],
            device_id={"gy": z + 1 if way == 0 else z - 1},
            device_id_type=MESH,
        )

    def send_own(index):
        kind, c = chunks[index]
        source = g_in if kind == "g" else h_in

        @pl.when(z < n_gy - 1)
        def _():
            chain_copy(kind, c, 0, z, source).start()

        @pl.when(z > 0)
        def _():
            chain_copy(kind, c, 1, z, source).start()

    def forward(index):
        kind, c = chunks[index]
        for s in range(1, n_gy):
            @pl.when(z - s >= 0)
            def _():
                copy = chain_copy(kind, c, 0, z - s)
                copy.wait_recv()

                @pl.when(z < n_gy - 1)
                def _():
                    copy.start()

            @pl.when(z + s <= n_gy - 1)
            def _():
                copy = chain_copy(kind, c, 1, z + s)
                copy.wait_recv()

                @pl.when(z > 0)
                def _():
                    copy.start()

    def drain(index):
        kind, c = chunks[index]
        for s in range(n_gy):
            @pl.when((z - s >= 0) & (z < n_gy - 1))
            def _():
                chain_copy(kind, c, 0, z - s).wait_send()

            @pl.when((z + s <= n_gy - 1) & (z > 0))
            def _():
                chain_copy(kind, c, 1, z + s).wait_send()

    def cross_gather(s, source, buf, send, recv, arrived=False):
        slot = 2 * lax.rem(chip - s + n_chips, n_chips) + core if arrived else gx
        return pltpu.make_async_remote_copy(
            src_ref=source, dst_ref=buf.at[slot], send_sem=send.at[s - 1], recv_sem=recv.at[s - 1],
            device_id={"gx": peer(s)}, device_id_type=MESH,
        )

    def core_gather(s, source, buf, send, recv):
        slot = 2 * lax.rem(chip - s + n_chips, n_chips) + core
        index = n_chips - 1 + s
        return pltpu.make_async_remote_copy(
            src_ref=buf.at[slot] if source is None else source,
            dst_ref=buf.at[slot], send_sem=send.at[index], recv_sem=recv.at[index],
            device_id={"gx": partner}, device_id_type=MESH,
        )

    def start_gather(source, buf, send, recv):
        for s in range(1, n_chips):
            cross_gather(s, source, buf, send, recv).start()
        core_gather(0, source, buf, send, recv).start()

    def pass_gather(source, buf, send, recv):
        for s in range(1, n_chips):
            cross_gather(s, source, buf, send, recv, True).wait_recv()
            core_gather(s, None, buf, send, recv).start()

    def end_gather(source, buf, send, recv):
        core_gather(0, source, buf, send, recv).wait()
        for s in range(1, n_chips):
            cross_gather(s, source, buf, send, recv).wait_send()
            core_gather(s, None, buf, send, recv).wait()

    def transpose_into(buf, out, pieces):
        width = buf.shape[2] // pieces

        @pl.loop(0, pieces)
        def _(i):
            columns = pl.ds(pl.multiple_of(i * width, width), width)
            block = buf[:, :, columns].reshape(tokens, width)
            out[columns, :] = block.T

    def multiply(index):
        kind, c = chunks[index]
        if kind == "g":
            buf, weight, load, acc, width = gall, wv, loads_w, acc_x, g_width
        else:
            buf, weight, load, acc, width = hall, mv, loads_m, acc_c, h_width
        load[c].wait()
        outs = acc.shape[1]
        tile = min(512, outs // 2)
        left = buf[:, :, c * width:(c + 1) * width].reshape(tokens, width)

        @pl.loop(0, outs // tile)
        def _(i):
            at = pl.ds(pl.multiple_of(i * tile, tile), tile)
            product = lax.dot_general(
                left, weight[c, at, :], (((1,), (1,)), ((), ())), preferred_element_type=F32
            )
            if c == 0:
                acc[:, at] = product
            else:
                acc[:, at] += product

    def to_partner(k, term, part, send, recv):
        return pltpu.make_async_remote_copy(
            src_ref=term.at[2 * k + 1 - core], dst_ref=part.at[k],
            send_sem=send.at[k], recv_sem=recv.at[k],
            device_id={"gx": partner}, device_id_type=MESH,
        )

    def to_chip(s, pair, cross, send, recv):
        return pltpu.make_async_remote_copy(
            src_ref=pair.at[s - 1], dst_ref=cross.at[s - 1],
            send_sem=send.at[s - 1], recv_sem=recv.at[s - 1],
            device_id={"gx": peer(s)}, device_id_type=MESH,
        )

    def scatter_first(acc, term, part, send, recv):
        size = acc.shape[0] // n_gx
        for b in range(n_gx):
            term[b] = acc[b * size:(b + 1) * size, :].astype(BF16)
        for k in range(n_chips):
            to_partner(k, term, part, send, recv).start()

    def scatter_second(term, part, send, recv, pair, cross, send2, recv2):
        for k in range(n_chips):
            to_partner(k, term, part, send, recv).wait()
        for s in range(1, n_chips):
            k = lax.rem(chip + s, n_chips)
            pair[s - 1] = (term[2 * k + core].astype(F32) + part[k].astype(F32)).astype(BF16)
            to_chip(s, pair, cross, send2, recv2).start()

    def scatter_last(term, part, pair, cross, send2, recv2, res):
        for s in range(1, n_chips):
            to_chip(s, pair, cross, send2, recv2).wait()
        total = term[gx].astype(F32) + part[chip].astype(F32)
        for s in range(1, n_chips):
            total = total + cross[s - 1].astype(F32)
        res[...] = total.astype(BF16)

    outs = [
        pltpu.make_async_copy(gall, gall_out, out_sem.at[0]),
        pltpu.make_async_copy(hall, hall_out, out_sem.at[1]),
        pltpu.make_async_copy(xt, xt_out, out_sem.at[2]),
        pltpu.make_async_copy(ct, ct_out, out_sem.at[3]),
        pltpu.make_async_copy(res_x, dx_out, out_sem.at[4]),
        pltpu.make_async_copy(res_c, dc_out, out_sem.at[5]),
    ]
    x_gather = (x_in, xall, xs_send, xs_recv)
    c_gather = (c_in, call, cs_send, cs_recv)

    for index in range(AHEAD):
        send_own(index)
    start_gather(*x_gather)
    start_gather(*c_gather)
    for copy in own:
        copy.wait()
    for index in range(len(chunks)):
        forward(index)
        if index + AHEAD < len(chunks):
            send_own(index + AHEAD)
        multiply(index)
        after = index - g_chunks + 1
        if after == -1:
            pass_gather(*x_gather)
            pass_gather(*c_gather)
        if after == 0:
            outs[0].start()
            scatter_first(acc_x, term_x, part_x, px_send, px_recv)
            end_gather(*x_gather)
            transpose_into(xall, xt, 8)
            outs[2].start()
        if after == 1:
            scatter_second(term_x, part_x, px_send, px_recv, pair_x, cross_x, cx_send, cx_recv)
            end_gather(*c_gather)
            transpose_into(call, ct, 4)
            outs[3].start()
    outs[1].start()
    scatter_first(acc_c, term_c, part_c, pc_send, pc_recv)
    scatter_last(term_x, part_x, pair_x, cross_x, cx_send, cx_recv, res_x)
    outs[4].start()
    scatter_second(term_c, part_c, pc_send, pc_recv, pair_c, cross_c, cc_send, cc_recv)
    for index in range(len(chunks)):
        drain(index)
    scatter_last(term_c, part_c, pair_c, cross_c, cc_send, cc_recv, res_c)
    outs[5].start()
    for copy in outs:
        copy.wait()


def exchange(n_gx, n_gy, x, w, g, c, m, h):
    g_chunks, h_chunks = 5, 4
    rows_g, rows_x = g.shape[0], x.shape[0]
    d, fp, ck, fm = x.shape[1], g.shape[1], c.shape[1], h.shape[1]
    tokens = rows_g * n_gy
    nc = n_gx // 2
    more = max(nc - 1, 1)
    dma = pltpu.SemaphoreType.DMA
    vm = pltpu.VMEM

    def scatter(width):
        return [
            vm((n_gx, rows_x, width), BF16), vm((nc, rows_x, width), BF16),
            vm((more, rows_x, width), BF16), vm((more, rows_x, width), BF16),
            vm((rows_x, width), BF16),
        ]

    shape = jax.ShapeDtypeStruct
    flops = 2 * tokens * (d * fp + ck * fm)
    return pl.pallas_call(
        functools.partial(exchange_kernel, n_gx, n_gy, g_chunks, h_chunks),
        out_shape=(
            shape((d, tokens), BF16), shape((ck, tokens), BF16),
            shape((n_gy, rows_g, fp), BF16), shape((n_gy, rows_g, fm), BF16),
            shape((rows_x, d), BF16), shape((rows_x, ck), BF16),
        ),
        in_specs=[pl.BlockSpec(memory_space=ANY)] * 6,
        out_specs=[pl.BlockSpec(memory_space=ANY)] * 6,
        scratch_shapes=[
            vm((g_chunks, d, fp // g_chunks), BF16), vm((h_chunks, ck, fm // h_chunks), BF16),
            vm((n_gy, rows_g, fp), BF16), vm((n_gy, rows_g, fm), BF16),
            vm((n_gx, rows_x, d), BF16), vm((n_gx, rows_x, ck), BF16),
            vm((d, tokens), BF16), vm((ck, tokens), BF16),
            vm((tokens, d), F32), vm((tokens, ck), F32),
            *scatter(d), *scatter(ck),
            dma((g_chunks,)), dma((h_chunks,)), dma((4,)),
            dma((2, n_gy, g_chunks)), dma((n_gy, g_chunks)),
            dma((2, n_gy, h_chunks)), dma((n_gy, h_chunks)),
            dma((2 * nc - 1,)), dma((2 * nc - 1,)), dma((2 * nc - 1,)), dma((2 * nc - 1,)),
            dma((nc,)), dma((nc,)), dma((more,)), dma((more,)),
            dma((nc,)), dma((nc,)), dma((more,)), dma((more,)),
            dma((6,)),
        ],
        compiler_params=pltpu.CompilerParams(
            collective_id=0, has_side_effects=True, vmem_limit_bytes=61 * 1024 * 1024
        ),
        cost_estimate=pl.CostEstimate(flops=flops, bytes_accessed=2 * (d * fp + ck * fm), transcendentals=0),
        name="exchange",
    )(x, w, g, c, m, h)


SLOTS = 3


def gradients_kernel(g_steps, h_steps, xt, ct, gall, hall, dw, dm, xv, cv, gv, hv, wbuf, mbuf, in_sem, w_sem, m_sem):
    first = [
        pltpu.make_async_copy(gall, gv, in_sem.at[0]),
        pltpu.make_async_copy(xt, xv, in_sem.at[1]),
        pltpu.make_async_copy(hall, hv, in_sem.at[2]),
        pltpu.make_async_copy(ct, cv, in_sem.at[3]),
    ]
    for copy in first:
        copy.start()

    def run(steps, pieces, left, right, buf, sem, out):
        tall = out.shape[0] // steps
        wide = out.shape[1] // pieces

        def copy_out(i, slot):
            at = pl.ds(pl.multiple_of(i * tall, tall), tall)
            return pltpu.make_async_copy(buf.at[slot], out.at[at, :], sem.at[slot])

        @pl.loop(0, steps)
        def _(i):
            slot = lax.rem(i, SLOTS)

            @pl.when(i >= SLOTS)
            def _():
                copy_out(i - SLOTS, slot).wait()

            part = left[pl.ds(pl.multiple_of(i * tall, tall), tall), :]
            for p in range(pieces):
                columns = slice(p * wide, (p + 1) * wide)
                buf[slot, :, columns] = jnp.dot(
                    part, right[:, columns], preferred_element_type=F32
                ).astype(BF16)
            copy_out(i, slot).start()

        return [copy_out(i, i % SLOTS) for i in range(max(steps - SLOTS, 0), steps)]

    first[0].wait()
    first[1].wait()
    last = run(g_steps, 5, xv, gv, wbuf, w_sem, dw)
    first[2].wait()
    first[3].wait()
    last += run(h_steps, 4, cv, hv, mbuf, m_sem, dm)
    for copy in last:
        copy.wait()


def gradients(xt, ct, gall, hall):
    g_steps, h_steps = 8, 4
    d, tokens = xt.shape
    ck = ct.shape[0]
    fp, fm = gall.shape[1], hall.shape[1]
    dma = pltpu.SemaphoreType.DMA
    vm = pltpu.VMEM
    shape = jax.ShapeDtypeStruct
    return pl.pallas_call(
        functools.partial(gradients_kernel, g_steps, h_steps),
        out_shape=(shape((d, fp), BF16), shape((ck, fm), BF16)),
        in_specs=[pl.BlockSpec(memory_space=ANY)] * 4,
        out_specs=[pl.BlockSpec(memory_space=ANY)] * 2,
        scratch_shapes=[
            vm((d, tokens), BF16), vm((ck, tokens), BF16), vm((tokens, fp), BF16), vm((tokens, fm), BF16),
            vm((SLOTS, d // g_steps, fp), BF16), vm((SLOTS, ck // h_steps, fm), BF16),
            dma((4,)), dma((SLOTS,)), dma((SLOTS,)),
        ],
        compiler_params=pltpu.CompilerParams(vmem_limit_bytes=60 * 1024 * 1024),
        cost_estimate=pl.CostEstimate(
            flops=2 * tokens * (d * fp + ck * fm), bytes_accessed=2 * (d * fp + ck * fm), transcendentals=0
        ),
        name="gradients",
    )(xt, ct, gall, hall)


def body(n_gx, n_gy, layer_input, packed_weight, packed_cotangent, context, mixing_weight, mixing_cotangent):
    xt, ct, gall, hall, dx, dc = exchange(
        n_gx, n_gy, layer_input, packed_weight, packed_cotangent, context, mixing_weight, mixing_cotangent
    )
    tokens = xt.shape[1]
    dw, dm = gradients(xt, ct, gall.reshape(tokens, -1), hall.reshape(tokens, -1))
    return dx, dw, dc, dm


def solution(mesh):
    return jax.shard_map(
        functools.partial(body, mesh.shape["gx"], mesh.shape["gy"]),
        mesh=mesh,
        in_specs=(
            P(("groups", "gx"), "gy"),
            P("gy", "gx"),
            P(("groups", "gy"), "gx"),
            P(("groups", "gx"), "gy"),
            P("gy", "gx"),
            P(("groups", "gy"), "gx"),
        ),
        out_specs=(
            P(("groups", "gx"), "gy"),
            P(("groups", "gy"), "gx"),
            P(("groups", "gx"), "gy"),
            P(("groups", "gy"), "gx"),
        ),
        check_vma=False,
    )
```

```python
import functools

import jax
import jax.numpy as jnp
from jax import lax
from jax.experimental import pallas as pl
from jax.experimental.pallas import tpu as pltpu
from jax.sharding import PartitionSpec as P

BF16 = jnp.bfloat16
F32 = jnp.float32
MESH = pl.DeviceIdType.MESH
ANY = pl.ANY
AHEAD = 3
TILE = 2048


def exchange_kernel(
    n_gx, n_gy, g_chunks, h_chunks,
    x_in, w_in, g_in, c_in, m_in, h_in,
    xt_out, ct_out, gall_out, hall_out, dx_out, dc_out,
    wv, mv, gall, hall, xall, call, xt, ct, acc_x, acc_c, flip,
    term_x, part_x, pair_x, cross_x, res_x,
    term_c, part_c, pair_c, cross_c, res_c,
    w_sem, m_sem, own_sem, g_send, g_recv, h_send, h_recv,
    xs_send, xs_recv, cs_send, cs_recv,
    px_send, px_recv, cx_send, cx_recv, pc_send, pc_recv, cc_send, cc_recv,
    out_sem,
):
    gx = lax.axis_index("gx")
    z = lax.axis_index("gy")
    core = lax.rem(gx, 2)
    chip = gx // 2
    partner = gx + 1 - 2 * core
    n_chips = n_gx // 2
    g_width = g_in.shape[1] // g_chunks
    h_width = h_in.shape[1] // h_chunks
    rows = g_in.shape[0]
    tokens = rows * n_gy

    def peer(s):
        return 2 * lax.rem(chip + s, n_chips) + core

    loads_w = [
        pltpu.make_async_copy(w_in.at[:, pl.ds(c * g_width, g_width)], wv.at[c], w_sem.at[c])
        for c in range(g_chunks)
    ]
    loads_m = [
        pltpu.make_async_copy(m_in.at[:, pl.ds(c * h_width, h_width)], mv.at[c], m_sem.at[c])
        for c in range(h_chunks)
    ]
    own = [
        pltpu.make_async_copy(x_in, xall.at[gx], own_sem.at[0]),
        pltpu.make_async_copy(c_in, call.at[gx], own_sem.at[1]),
    ]
    own_blocks = [
        pltpu.make_async_copy(g_in.at[:, pl.ds(c * g_width, g_width)], gall.at[c, z], own_sem.at[2 + c])
        for c in range(g_chunks)
    ] + [
        pltpu.make_async_copy(h_in.at[:, pl.ds(c * h_width, h_width)], hall.at[c, z], own_sem.at[2 + g_chunks + c])
        for c in range(h_chunks)
    ]
    for copy in own_blocks + own:
        copy.start()
    for copy in loads_w:
        copy.start()
    for copy in loads_m:
        copy.start()

    barrier = pltpu.get_barrier_semaphore()

    def greet(**where):
        pl.semaphore_signal(barrier, inc=1, device_id=where, device_id_type=MESH)

    greet(gx=partner)
    for s in range(1, n_chips):
        greet(gx=peer(s))

    ends = 0
    for hops in (1, 2):
        @pl.when(z - hops >= 0)
        def _():
            greet(gy=z - hops)

        @pl.when(z + hops < n_gy)
        def _():
            greet(gy=z + hops)

        ends += jnp.where(z - hops >= 0, 1, 0) + jnp.where(z + hops < n_gy, 1, 0)

    pl.semaphore_wait(barrier, n_chips + ends)

    chunks = [("g", c) for c in range(g_chunks)] + [("h", c) for c in range(h_chunks)]

    def chain_copy(kind, c, way, block, hops=1):
        buf, send, recv = (gall, g_send, g_recv) if kind == "g" else (hall, h_send, h_recv)
        return pltpu.make_async_remote_copy(
            src_ref=buf.at[c, block],
            dst_ref=buf.at[c, block],
            send_sem=send.at[way + 2 * (hops - 1), block, c],
            recv_sem=recv.at[block, c],
            device_id={"gy": z + hops if way == 0 else z - hops},
            device_id_type=MESH,
        )

    def send_own(index):
        kind, c = chunks[index]
        own_blocks[index].wait()

        for hops in (2, 1):
            @pl.when(z + hops < n_gy)
            def _():
                chain_copy(kind, c, 0, z, hops).start()

            @pl.when(z - hops >= 0)
            def _():
                chain_copy(kind, c, 1, z, hops).start()

    def forward(index):
        kind, c = chunks[index]
        for s in range(1, n_gy):
            @pl.when(z - s >= 0)
            def _():
                copy = chain_copy(kind, c, 0, z - s)
                copy.wait_recv()
                if s >= 2:
                    @pl.when(z < n_gy - 1)
                    def _():
                        copy.start()

            @pl.when(z + s <= n_gy - 1)
            def _():
                copy = chain_copy(kind, c, 1, z + s)
                copy.wait_recv()
                if s >= 2:
                    @pl.when(z > 0)
                    def _():
                        copy.start()

    def drain(index):
        kind, c = chunks[index]
        for hops in (1, 2):
            @pl.when(z + hops < n_gy)
            def _():
                chain_copy(kind, c, 0, z, hops).wait_send()

            @pl.when(z - hops >= 0)
            def _():
                chain_copy(kind, c, 1, z, hops).wait_send()

        for s in range(2, n_gy):
            @pl.when((z - s >= 0) & (z < n_gy - 1))
            def _():
                chain_copy(kind, c, 0, z - s).wait_send()

            @pl.when((z + s <= n_gy - 1) & (z > 0))
            def _():
                chain_copy(kind, c, 1, z + s).wait_send()

    def cross_gather(s, source, buf, send, recv, arrived=False):
        slot = 2 * lax.rem(chip - s + n_chips, n_chips) + core if arrived else gx
        return pltpu.make_async_remote_copy(
            src_ref=source, dst_ref=buf.at[slot], send_sem=send.at[s - 1], recv_sem=recv.at[s - 1],
            device_id={"gx": peer(s)}, device_id_type=MESH,
        )

    def core_gather(s, source, buf, send, recv):
        slot = 2 * lax.rem(chip - s + n_chips, n_chips) + core
        index = n_chips - 1 + s
        return pltpu.make_async_remote_copy(
            src_ref=buf.at[slot] if source is None else source,
            dst_ref=buf.at[slot], send_sem=send.at[index], recv_sem=recv.at[index],
            device_id={"gx": partner}, device_id_type=MESH,
        )

    def start_gather(source, buf, send, recv):
        for s in range(1, n_chips):
            cross_gather(s, source, buf, send, recv).start()
        core_gather(0, source, buf, send, recv).start()

    def pass_gather(source, buf, send, recv):
        for s in range(1, n_chips):
            cross_gather(s, source, buf, send, recv, True).wait_recv()
            core_gather(s, None, buf, send, recv).start()

    def end_gather(source, buf, send, recv):
        core_gather(0, source, buf, send, recv).wait()
        for s in range(1, n_chips):
            cross_gather(s, source, buf, send, recv).wait_send()
            core_gather(s, None, buf, send, recv).wait()

    def transpose_into(buf, out, pieces):
        width = buf.shape[2] // pieces

        @pl.loop(0, pieces)
        def _(i):
            columns = pl.ds(pl.multiple_of(i * width, width), width)
            block = buf[:, :, columns].reshape(tokens, width)
            out[columns, :] = block.T

    def multiply(index):
        kind, c = chunks[index]
        if kind == "g":
            buf, weight, load, acc, width = gall, wv, loads_w, acc_x, g_width
        else:
            buf, weight, load, acc, width = hall, mv, loads_m, acc_c, h_width
        load[c].wait()
        outs = acc.shape[0]
        tile = min(TILE, outs)
        flip[:width, :] = buf[c].reshape(tokens, width).T

        @pl.loop(0, outs // tile)
        def _(i):
            at = pl.ds(pl.multiple_of(i * tile, tile), tile)
            product = jnp.dot(weight[c, at, :], flip[:width, :], preferred_element_type=F32)
            if c == 0:
                acc[at, :] = product
            else:
                acc[at, :] += product

    def to_partner(k, term, part, send, recv):
        return pltpu.make_async_remote_copy(
            src_ref=term.at[2 * k + 1 - core], dst_ref=part.at[k],
            send_sem=send.at[k], recv_sem=recv.at[k],
            device_id={"gx": partner}, device_id_type=MESH,
        )

    def to_chip(s, pair, cross, send, recv):
        return pltpu.make_async_remote_copy(
            src_ref=pair.at[s - 1], dst_ref=cross.at[s - 1],
            send_sem=send.at[s - 1], recv_sem=recv.at[s - 1],
            device_id={"gx": peer(s)}, device_id_type=MESH,
        )

    def scatter_first(acc, term, part, send, recv):
        width = min(512, acc.shape[0] // 2)

        @pl.loop(0, acc.shape[0] // width)
        def _(i):
            at = pl.ds(pl.multiple_of(i * width, width), width)
            block = acc[at, :].astype(BF16).T
            term[:, :, at] = block.reshape(n_gx, tokens // n_gx, width)

        for k in range(n_chips):
            to_partner(k, term, part, send, recv).start()

    def scatter_second(term, part, send, recv, pair, cross, send2, recv2):
        for k in range(n_chips):
            to_partner(k, term, part, send, recv).wait()
        for s in range(1, n_chips):
            k = lax.rem(chip + s, n_chips)
            pair[s - 1] = (term[2 * k + core].astype(F32) + part[k].astype(F32)).astype(BF16)
            to_chip(s, pair, cross, send2, recv2).start()

    def scatter_last(term, part, pair, cross, send2, recv2, res):
        for s in range(1, n_chips):
            to_chip(s, pair, cross, send2, recv2).wait()
        total = term[gx].astype(F32) + part[chip].astype(F32)
        for s in range(1, n_chips):
            total = total + cross[s - 1].astype(F32)
        res[...] = total.astype(BF16)

    outs = [
        pltpu.make_async_copy(gall, gall_out, out_sem.at[0]),
        pltpu.make_async_copy(hall, hall_out, out_sem.at[1]),
        pltpu.make_async_copy(xt, xt_out, out_sem.at[2]),
        pltpu.make_async_copy(ct, ct_out, out_sem.at[3]),
        pltpu.make_async_copy(res_x, dx_out, out_sem.at[4]),
        pltpu.make_async_copy(res_c, dc_out, out_sem.at[5]),
    ]
    x_gather = (x_in, xall, xs_send, xs_recv)
    c_gather = (c_in, call, cs_send, cs_recv)

    for index in range(AHEAD):
        send_own(index)
    start_gather(*x_gather)
    start_gather(*c_gather)
    for copy in own:
        copy.wait()
    for index in range(len(chunks)):
        forward(index)
        if index + AHEAD < len(chunks):
            send_own(index + AHEAD)
        multiply(index)
        after = index - g_chunks + 1
        if after == -1:
            pass_gather(*x_gather)
            pass_gather(*c_gather)
        if after == 0:
            outs[0].start()
            scatter_first(acc_x, term_x, part_x, px_send, px_recv)
            end_gather(*x_gather)
            transpose_into(xall, xt, 8)
            outs[2].start()
        if after == 1:
            scatter_second(term_x, part_x, px_send, px_recv, pair_x, cross_x, cx_send, cx_recv)
            end_gather(*c_gather)
            transpose_into(call, ct, 4)
            outs[3].start()
    outs[1].start()
    scatter_first(acc_c, term_c, part_c, pc_send, pc_recv)
    scatter_last(term_x, part_x, pair_x, cross_x, cx_send, cx_recv, res_x)
    outs[4].start()
    scatter_second(term_c, part_c, pc_send, pc_recv, pair_c, cross_c, cc_send, cc_recv)
    for index in range(len(chunks)):
        drain(index)
    scatter_last(term_c, part_c, pair_c, cross_c, cc_send, cc_recv, res_c)
    outs[5].start()
    for copy in outs:
        copy.wait()


def exchange(n_gx, n_gy, x, w, g, c, m, h):
    g_chunks, h_chunks = (2 if g.shape[1] % 256 == 0 else 5), 4
    rows_g, rows_x = g.shape[0], x.shape[0]
    d, fp, ck, fm = x.shape[1], g.shape[1], c.shape[1], h.shape[1]
    tokens = rows_g * n_gy
    nc = n_gx // 2
    more = max(nc - 1, 1)
    dma = pltpu.SemaphoreType.DMA
    vm = pltpu.VMEM

    def scatter(width):
        return [
            vm((n_gx, rows_x, width), BF16), vm((nc, rows_x, width), BF16),
            vm((more, rows_x, width), BF16), vm((more, rows_x, width), BF16),
            vm((rows_x, width), BF16),
        ]

    shape = jax.ShapeDtypeStruct
    flops = 2 * tokens * (d * fp + ck * fm)
    return pl.pallas_call(
        functools.partial(exchange_kernel, n_gx, n_gy, g_chunks, h_chunks),
        out_shape=(
            shape((d, tokens), BF16), shape((ck, tokens), BF16),
            shape((g_chunks, n_gy, rows_g, fp // g_chunks), BF16), shape((h_chunks, n_gy, rows_g, fm // h_chunks), BF16),
            shape((rows_x, d), BF16), shape((rows_x, ck), BF16),
        ),
        in_specs=[pl.BlockSpec(memory_space=ANY)] * 6,
        out_specs=[pl.BlockSpec(memory_space=ANY)] * 6,
        scratch_shapes=[
            vm((g_chunks, d, fp // g_chunks), BF16), vm((h_chunks, ck, fm // h_chunks), BF16),
            vm((g_chunks, n_gy, rows_g, fp // g_chunks), BF16), vm((h_chunks, n_gy, rows_g, fm // h_chunks), BF16),
            vm((n_gx, rows_x, d), BF16), vm((n_gx, rows_x, ck), BF16),
            vm((d, tokens), BF16), vm((ck, tokens), BF16),
            vm((d, tokens), F32), vm((ck, tokens), F32),
            vm((max(fp // g_chunks, fm // h_chunks), tokens), BF16),
            *scatter(d), *scatter(ck),
            dma((g_chunks,)), dma((h_chunks,)), dma((2 + g_chunks + h_chunks,)),
            dma((4, n_gy, g_chunks)), dma((n_gy, g_chunks)),
            dma((4, n_gy, h_chunks)), dma((n_gy, h_chunks)),
            dma((2 * nc - 1,)), dma((2 * nc - 1,)), dma((2 * nc - 1,)), dma((2 * nc - 1,)),
            dma((nc,)), dma((nc,)), dma((more,)), dma((more,)),
            dma((nc,)), dma((nc,)), dma((more,)), dma((more,)),
            dma((6,)),
        ],
        compiler_params=pltpu.CompilerParams(
            collective_id=0, has_side_effects=True, vmem_limit_bytes=61 * 1024 * 1024
        ),
        cost_estimate=pl.CostEstimate(flops=flops, bytes_accessed=2 * (d * fp + ck * fm), transcendentals=0),
        name="exchange",
    )(x, w, g, c, m, h)


SLOTS = 3


def gradients_kernel(
    g_steps, h_steps, xt, ct, gall, hall, dx, dc, dw, dm, dx_out, dc_out,
    xv, cv, gv, hv, dxv, dcv, wbuf, mbuf, in_sem, w_sem, m_sem,
):
    head = xt.shape[0] // g_steps
    rest = pl.ds(head, xt.shape[0] - head)
    first = [
        pltpu.make_async_copy(gall, gv, in_sem.at[0]),
        pltpu.make_async_copy(xt.at[pl.ds(0, head), :], xv.at[pl.ds(0, head), :], in_sem.at[1]),
        pltpu.make_async_copy(xt.at[rest, :], xv.at[rest, :], in_sem.at[4]),
        pltpu.make_async_copy(hall, hv, in_sem.at[2]),
        pltpu.make_async_copy(ct, cv, in_sem.at[3]),
        pltpu.make_async_copy(dx, dxv, in_sem.at[5]),
        pltpu.make_async_copy(dc, dcv, in_sem.at[6]),
    ]
    for copy in first:
        copy.start()

    def run(steps, left, right, buf, sem, out, late=None):
        tall = out.shape[0] // steps
        pieces, _, wide = right.shape

        def copy_out(i, slot):
            at = pl.ds(pl.multiple_of(i * tall, tall), tall)
            return pltpu.make_async_copy(buf.at[slot], out.at[at, :], sem.at[slot])

        @pl.loop(0, steps)
        def _(i):
            slot = lax.rem(i, SLOTS)

            @pl.when(i >= SLOTS)
            def _():
                copy_out(i - SLOTS, slot).wait()

            if late is not None:
                @pl.when(i == 1)
                def _():
                    late.wait()

            part = left[pl.ds(pl.multiple_of(i * tall, tall), tall), :]
            for p in range(pieces):
                columns = slice(p * wide, (p + 1) * wide)
                buf[slot, :, columns] = jnp.dot(
                    part, right[p], preferred_element_type=F32
                ).astype(BF16)
            copy_out(i, slot).start()

        return [copy_out(i, i % SLOTS) for i in range(max(steps - SLOTS, 0), steps)]

    first[0].wait()
    first[1].wait()
    last = run(g_steps, xv, gv, wbuf, w_sem, dw, first[2])
    for copy in first[3:]:
        copy.wait()
    small = [
        pltpu.make_async_copy(dxv, dx_out, in_sem.at[5]),
        pltpu.make_async_copy(dcv, dc_out, in_sem.at[6]),
    ]
    for copy in small:
        copy.start()
    last += run(h_steps, cv, hv, mbuf, m_sem, dm)
    for copy in last + small:
        copy.wait()


def gradients(xt, ct, gall, hall, dx, dc):
    g_steps, h_steps = 8, 4
    d, tokens = xt.shape
    ck = ct.shape[0]
    fp, fm = gall.shape[0] * gall.shape[2], hall.shape[0] * hall.shape[2]
    dma = pltpu.SemaphoreType.DMA
    vm = pltpu.VMEM
    shape = jax.ShapeDtypeStruct
    return pl.pallas_call(
        functools.partial(gradients_kernel, g_steps, h_steps),
        out_shape=(shape((d, fp), BF16), shape((ck, fm), BF16), shape(dx.shape, BF16), shape(dc.shape, BF16)),
        in_specs=[pl.BlockSpec(memory_space=ANY)] * 6,
        out_specs=[pl.BlockSpec(memory_space=ANY)] * 4,
        scratch_shapes=[
            vm((d, tokens), BF16), vm((ck, tokens), BF16), vm(gall.shape, BF16), vm(hall.shape, BF16), vm(dx.shape, BF16), vm(dc.shape, BF16),
            vm((SLOTS, d // g_steps, fp), BF16), vm((SLOTS, ck // h_steps, fm), BF16),
            dma((7,)), dma((SLOTS,)), dma((SLOTS,)),
        ],
        compiler_params=pltpu.CompilerParams(vmem_limit_bytes=60 * 1024 * 1024),
        cost_estimate=pl.CostEstimate(
            flops=2 * tokens * (d * fp + ck * fm), bytes_accessed=2 * (d * fp + ck * fm), transcendentals=0
        ),
        name="gradients",
    )(xt, ct, gall, hall, dx, dc)


def body(n_gx, n_gy, layer_input, packed_weight, packed_cotangent, context, mixing_weight, mixing_cotangent):
    xt, ct, gall, hall, dx, dc = exchange(
        n_gx, n_gy, layer_input, packed_weight, packed_cotangent, context, mixing_weight, mixing_cotangent
    )
    tokens = xt.shape[1]
    gall = gall.reshape(gall.shape[0], tokens, -1)
    hall = hall.reshape(hall.shape[0], tokens, -1)
    dw, dm, dx, dc = gradients(xt, ct, gall, hall, dx, dc)
    return dx, dw, dc, dm


def solution(mesh):
    return jax.shard_map(
        functools.partial(body, mesh.shape["gx"], mesh.shape["gy"]),
        mesh=mesh,
        in_specs=(
            P(("groups", "gx"), "gy"),
            P("gy", "gx"),
            P(("groups", "gy"), "gx"),
            P(("groups", "gx"), "gy"),
            P("gy", "gx"),
            P(("groups", "gy"), "gx"),
        ),
        out_specs=(
            P(("groups", "gx"), "gy"),
            P(("groups", "gy"), "gx"),
            P(("groups", "gx"), "gy"),
            P(("groups", "gy"), "gx"),
        ),
        check_vma=False,
    )
```
